512 devices in a mesh: stratum: 16 (over y, z_hi), user: 32 (over x, z_lo, core).
Axes of the slice: x: 4, y: 8, z: 8 (z_hi: 2, z_lo: 4; z = z_hi * 4 + z_lo), core: 2. Of those that a mesh axis runs over, the one named last changes fastest.
Arguments:
- users: bfloat16 [524288, 512], P(('stratum', 'user')), may hold values from -6 to 6
- items: float32 [4096, 512], P(('stratum', 'user')), may hold values from -6 to 6
- momentum: float32 [4096, 512], P(('stratum', 'user')), may hold values from -30 to 30
- ratings: bfloat16 [524288, 4, 256], P(('stratum', 'user')), may hold values from -6.25 to 6.25, as said below
Outputs:
- new_users: bfloat16 [524288, 512], P(('stratum', 'user'))
- new_items: float32 [4096, 512], P(('stratum', 'user'))
- new_momentum: float32 [4096, 512], P(('stratum', 'user'))
The draws below stay inside these ranges and needn't reach their ends.
Inputs may be any that keep to these rules, and one draw needn't show every extreme that they name: `ratings`: an entry equal to zero marks an unobserved rating; every observed rating has magnitude 0.25 or more.
All inputs are finite; a program needn't handle non-finite values.
Results may differ from the reference program's by a relative error of at most 0.013.
The reference program's roundings to bfloat16 on the way count: a program that leaves them out, or rounds other values in their place, can miss the bound.
Values may be sent and summed in bfloat16 or wider, within the bound.
A program may use at most 64 MiB of HBM per device.

```python
import jax
import jax.numpy as jnp
from jax import lax

R = 512
USR_DEV = 1024
ITEM_DEV = 8
STEPS = 4
ITEM_BLK = 256
USERS = 524288
ITEMS = 4096
N_STRATUM = 16
N_USER = 32


def draw_ratings(key, part):
    keys = jax.random.split(jax.random.fold_in(key, 7), 4)
    row_factor = jax.random.uniform(keys[0], (USERS, 1, 1), jnp.float32, 0.55, 1.0)
    col_factor = jax.random.uniform(keys[1], (1, STEPS, ITEM_BLK), jnp.float32, 0.6, 1.0)
    chance = jax.random.uniform(keys[2], (USERS, STEPS, ITEM_BLK), jnp.float32)
    observed = chance < row_factor * col_factor
    normal = jnp.clip(jax.random.normal(keys[3], (USERS, STEPS, ITEM_BLK), jnp.float32), -6.0, 6.0)
    values = jnp.where(normal >= 0, 0.25 + normal, -0.25 + normal)
    return jnp.where(observed, values, 0.0).astype(jnp.bfloat16)


def block_levels(own_key, extent, cuts, smallest, high):
    def one(dim, shards_of):
        heights = jax.random.uniform(jax.random.fold_in(jax.random.fold_in(own_key, 6), dim), (shards_of,), jnp.float32, smallest / len(cuts), high / len(cuts))
        return jnp.repeat(jnp.exp(heights), extent[dim] // shards_of).reshape((-1,) + (1,) * (len(extent) - dim - 1))

    factor_of = one(*cuts[0])
    for cut in cuts[1:]:
        factor_of = factor_of * one(*cut)
    return factor_of


def scatter_about(own_key, shape, spread, most, cuts=(), dtype=jnp.bfloat16):
    loudness = block_levels(own_key, shape, cuts, -0.22, 0.18) if cuts else 1.0
    drawn = jax.random.normal(own_key, shape, jnp.float32) * spread * loudness
    return jnp.minimum(jnp.maximum(drawn, -most), most).astype(dtype)


def setup_inputs(seed: int = 0) -> dict:
    seeds = jax.random.split(jax.random.key(seed), 5)
    users = scatter_about(seeds[0], (USERS, R), 1.0, 6.0, ((0, 512),))
    items = scatter_about(seeds[1], (ITEMS, R), 1.0, 6.0, ((0, 512),), jnp.float32)
    momentum = scatter_about(seeds[2], (ITEMS, R), 5.0, 30.0, ((0, 512),), jnp.float32)
    ratings = draw_ratings(jax.random.fold_in(seeds[4], 71), 0)
    return {"users": users, "items": items, "momentum": momentum, "ratings": ratings}


user_rate = 1.0
item_rate = 0.04
inertia = 0.6


def reference(users, items, momentum, ratings):
    strata = N_STRATUM
    user_rows = USR_DEV * N_USER
    block_rows = ITEM_DEV * N_USER
    factor = R ** -0.5
    ublock = users.reshape(strata, user_rows, R)
    vblock = items.reshape(strata, block_rows, R)
    mblock = momentum.reshape(strata, block_rows, R)
    tiles = ratings.reshape(strata, user_rows, STEPS, block_rows)

    def one_stratum(packed):
        urows, vrows, tile = packed
        weights = vrows.astype(jnp.bfloat16)
        score = jnp.dot(urows, weights.T, preferred_element_type=jnp.float32)
        resid = jnp.where(tile != 0, score * factor - tile.astype(jnp.float32), 0.0).astype(jnp.bfloat16)
        grads = jnp.dot(resid.T, urows, preferred_element_type=jnp.float32)
        change = jnp.dot(resid, weights, preferred_element_type=jnp.float32)
        fresh = (urows.astype(jnp.float32) - user_rate * factor * change).astype(jnp.bfloat16)
        return fresh, grads

    for step in range(STEPS):
        ublock, grads = lax.map(one_stratum, (ublock, vblock, tiles[:, :, step, :]))
        mblock = inertia * mblock + factor * grads
        vblock = vblock - item_rate * mblock
        vblock = jnp.roll(vblock, -1, 0)
        mblock = jnp.roll(mblock, -1, 0)
    return ublock.reshape(USERS, R), vblock.reshape(ITEMS, R), mblock.reshape(ITEMS, R)
```

```python
import functools

import jax
import jax.numpy as jnp
from jax import lax
from jax.experimental import pallas as pl
from jax.experimental.pallas import tpu as pltpu
from jax.sharding import PartitionSpec as P

R = 512
HALF = 256
STEPS = 4
USERS = 1024
BLOCK = 256
X = 4
Z = 4
CHIPS = 16
ROWS = 16
STRATA = 16
FACTOR = R**-0.5
user_rate = 1.0
item_rate = 0.04
inertia = 0.6

MESH = pl.DeviceIdType.MESH
NT = (((1,), (1,)), ((), ()))
NN = (((1,), (0,)), ((), ()))
TILE = 256


def dot(a, b, dims):
    return lax.dot_general(a, b, dims, preferred_element_type=jnp.float32)


def kernel(
    users_in,
    items_in,
    momentum_in,
    ratings_in,
    users_out,
    items_out,
    momentum_out,
    u,
    raw,
    x,
    wide0,
    wide1,
    own,
    first,
    w,
    score,
    e,
    et,
    g,
    give,
    take,
    part,
    parts,
    state,
    fresh,
    load_sem,
    ag_send,
    ag_recv,
    fw_send,
    fw_recv,
    sib_send,
    sib_recv,
    rs_send,
    rs_recv,
    st_send,
    st_recv,
):
    s = lax.axis_index("stratum")
    me = lax.axis_index("user")
    core = me % 2
    chip = me // 2
    mx, mz = chip // Z, chip % Z
    prev = (s + STRATA - 1) % STRATA
    nxt = (s + 1) % STRATA
    other = 1 - core

    def chip_at(dx, dz):
        return ((mx + dx) % X) * Z + (mz + dz) % Z

    def dev(k, c):
        return k * 2 + c

    loads = [
        pltpu.make_async_copy(items_in, own.at[0], load_sem.at[0]),
        pltpu.make_async_copy(momentum_in, own.at[1], load_sem.at[1]),
        pltpu.make_async_copy(ratings_in, raw, load_sem.at[2]),
        pltpu.make_async_copy(users_in.at[:, pl.ds(0, HALF)], u.at[0], load_sem.at[3]),
        pltpu.make_async_copy(users_in.at[:, pl.ds(HALF, HALF)], u.at[1], load_sem.at[4]),
    ]
    for copy in loads:
        copy.start()

    far = [(dx, dz) for dx in (2, 1, 3, 0) for dz in (2, 1, 3, 0)]
    barrier = pltpu.get_barrier_semaphore()

    def hello(stratum, user):
        pl.semaphore_signal(barrier, inc=1, device_id=(stratum, user), device_id_type=MESH)

    for dx, dz in far:
        k = chip_at(dx, dz)
        hello(prev, dev(k, core))
        hello(nxt, dev(k, core))
        if (dx, dz) != (0, 0):
            hello(s, dev(k, core))
    hello(prev, dev(chip, other))
    hello(nxt, dev(chip, other))
    hello(s, dev(chip, other))
    loads[0].wait()
    loads[1].wait()
    first[core, chip] = jnp.concatenate([own[0, :, :HALF], own[0, :, HALF:]], axis=0).astype(
        jnp.bfloat16
    )
    pl.semaphore_wait(barrier, 3 * CHIPS + 2)

    def remote(src, dst, send, recv, stratum, user):
        return pltpu.make_async_remote_copy(
            src_ref=src,
            dst_ref=dst,
            send_sem=send,
            recv_sem=recv,
            device_id=(stratum, user),
            device_id_type=MESH,
        )

    def rows_of(k):
        return pl.ds(pl.multiple_of(k * ROWS, ROWS), ROWS)

    def spread(t, place):
        sends = []
        mine = place(core, chip)
        for dx, dz in far[:-1]:
            k = chip_at(dx, dz)
            sends.append(
                remote(mine, mine, ag_send.at[t, dx * Z + dz], ag_recv.at[t, chip], s, dev(k, core))
            )
            sends[-1].start()
        passed = []

        def pass_on(k, slot):
            piece = place(core, k)
            passed.append(
                remote(piece, piece, fw_send.at[t, slot], fw_recv.at[t, k], s, dev(chip, other))
            )
            passed[-1].start()

        pass_on(chip, 0)
        return sends, passed, pass_on

    def collect(t, place, pass_on):
        for slot, (dx, dz) in enumerate(far[:-1][::-1]):
            k = chip_at(dx, dz)
            piece = place(core, k)
            remote(piece, piece, ag_send.at[t, 0], ag_recv.at[t, k], s, me).wait_recv()
            pass_on(k, slot + 1)

    def collect_passed(t, place):
        for dx, dz in far[::-1]:
            k = chip_at(dx, dz)
            piece = place(other, k)
            remote(piece, piece, fw_send.at[t, 0], fw_recv.at[t, k], s, me).wait_recv()

    def finish(sends):
        for copy in sends:
            copy.wait_send()

    def place_first(c, k):
        return first.at[c, k]

    sends, passed, pass_on = spread(0, place_first)
    moves = []
    for c in range(2):
        moves.append(
            remote(
                own.at[:, :, pl.ds(c * HALF, HALF)],
                state.at[0, :, pl.ds(pl.multiple_of(core * 8, 8), 8), :],
                st_send.at[0, c],
                st_recv.at[0, core],
                prev,
                dev(chip, c),
            )
        )
        moves[-1].start()

    loads[2].wait()

    def split(i, _):
        r = pl.ds(pl.multiple_of(i * 128, 128), 128)
        for h, wide in enumerate((wide0, wide1)):
            lanes = slice(h * 128, h * 128 + 128)
            wide[...] = raw[r, :, lanes].astype(jnp.float32).reshape(128 * STEPS, 128)
        for t in range(STEPS):
            for h, wide in enumerate((wide0, wide1)):
                lanes = slice(h * 128, h * 128 + 128)
                x[t, r, lanes] = wide[pl.ds(t, 128, stride=STEPS), :].astype(jnp.bfloat16)
        return 0

    lax.fori_loop(0, USERS // 128, split, 0)
    loads[3].wait()
    loads[4].wait()

    collect(0, place_first, pass_on)
    collect_passed(0, place_first)
    finish(sends + passed)
    pieces = [first[c].astype(jnp.float32).reshape(CHIPS, 2, 8, HALF) for c in range(2)]
    for h in range(2):
        w[0, h] = (
            jnp.concatenate([pieces[0][:, h : h + 1], pieces[1][:, h : h + 1]], axis=1)
            .reshape(BLOCK, HALF)
            .astype(jnp.bfloat16)
        )

    store = []
    for t in range(STEPS):
        last = t == STEPS - 1

        def place(c, k, t=t):
            return w.at[t, c, rows_of(k), :]

        tiles = [pl.ds(i * TILE, TILE) for i in range(USERS // TILE)]
        if t == 0:
            for r in tiles:
                score[r, :] = dot(u[core, r, :], w[t, core], NT)
        else:
            for r in tiles:
                score[r, :] = dot(u[core, r, :], w[t, core], NT)
            collect_passed(t, place)
            finish(sends + passed)
        for r in tiles:
            total = score[r, :] + dot(u[other, r, :], w[t, other], NT)
            tile = x[t, r, :].astype(jnp.float32)
            resid = jnp.where(tile != 0, total * FACTOR - tile, 0.0).astype(jnp.bfloat16)
            e[r, :] = resid
            et[:, r] = resid.T
        if last:
            for h in range(2):
                g[h] = dot(et[...], u[h], NN).reshape(CHIPS, 2, 8, HALF)

            def piece_for(c):
                both = [g[h, :, pl.ds(c, 1)] for h in range(2)]
                return jnp.concatenate(both, axis=1).reshape(BLOCK, HALF)

            give[t] = piece_for(other).astype(jnp.bfloat16)
        else:
            give[t] = dot(et[...], u[other], NN).astype(jnp.bfloat16)
        swap = remote(
            give.at[t], take.at[t], sib_send.at[t], sib_recv.at[t], s, dev(chip, other)
        )
        swap.start()
        if not last:
            g[0] = dot(et[...], u[core], NN).reshape(CHIPS, 2, 8, HALF)
        for h in range(2):
            for r in tiles:
                change = dot(e[r, :], w[t, h], NN)
                u[h, r, :] = (
                    u[h, r, :].astype(jnp.float32) - user_rate * FACTOR * change
                ).astype(jnp.bfloat16)
        if last:
            for h in range(2):
                store.append(
                    pltpu.make_async_copy(
                        u.at[h], users_out.at[:, pl.ds(h * HALF, HALF)], load_sem.at[3 + h]
                    )
                )
                store[-1].start()
        swap.wait_recv()
        mine = piece_for(core) if last else g[0].reshape(BLOCK, HALF)
        part[t] = (mine + take[t].astype(jnp.float32)).astype(jnp.bfloat16)
        gives = []
        for dx, dz in far:
            k = chip_at(dx, dz)
            gives.append(
                remote(
                    part.at[t, rows_of(k), :],
                    parts.at[t, chip],
                    rs_send.at[t, dx * Z + dz],
                    rs_recv.at[t, chip],
                    prev,
                    dev(k, core),
                )
            )
            gives[-1].start()
        if t == 0 or last:
            for c in range(2):
                remote(
                    own.at[:, :, pl.ds(c * HALF, HALF)],
                    state.at[t, :, pl.ds(c * 8, 8), :],
                    st_send.at[t, c],
                    st_recv.at[t, c],
                    s,
                    me,
                ).wait_recv()
        else:
            remote(
                fresh.at[t], state.at[t], st_send.at[t, 0], st_recv.at[t, 0], s, me
            ).wait_recv()
        for dx, dz in far[::-1]:
            k = chip_at(dx, dz)
            remote(
                part.at[t, rows_of(k), :], parts.at[t, k], rs_send.at[t, 0], rs_recv.at[t, k], s, me
            ).wait_recv()
        grads = jnp.sum(parts[t].astype(jnp.float32), axis=0)
        momentum = inertia * state[t, 1] + FACTOR * grads
        items = state[t, 0] - item_rate * momentum
        if last:
            for h in range(2):
                items_out[:, h * HALF : h * HALF + HALF] = items[h * 8 : h * 8 + 8]
                momentum_out[:, h * HALF : h * HALF + HALF] = momentum[h * 8 : h * 8 + 8]
        else:
            w[t + 1, core, rows_of(chip), :] = items.astype(jnp.bfloat16)

            def place(c, k, t=t + 1):
                return w.at[t, c, rows_of(k), :]

            sends, passed, pass_on = spread(t + 1, place)
            fresh[t, 0] = items
            fresh[t, 1] = momentum
            if t == STEPS - 2:
                for c in range(2):
                    moves.append(
                        remote(
                            fresh.at[t, :, pl.ds(c * 8, 8), :],
                            state.at[t + 1, :, pl.ds(pl.multiple_of(core * 8, 8), 8), :],
                            st_send.at[t + 1, c],
                            st_recv.at[t + 1, core],
                            prev,
                            dev(chip, c),
                        )
                    )
                    moves[-1].start()
            else:
                moves.append(
                    remote(
                        fresh.at[t],
                        state.at[t + 1],
                        st_send.at[t + 1, 0],
                        st_recv.at[t + 1, 0],
                        prev,
                        me,
                    )
                )
                moves[-1].start()
            collect(t + 1, place, pass_on)
        moves += [*gives, swap]
    finish(moves)
    for copy in store:
        copy.wait()


def local(users, items, momentum, ratings):
    bf16, f32 = jnp.bfloat16, jnp.float32
    any_space = pl.BlockSpec(memory_space=pl.ANY)
    vmem = pl.BlockSpec(memory_space=pltpu.VMEM)
    dma = pltpu.SemaphoreType.DMA
    return pl.pallas_call(
        kernel,
        out_shape=(
            jax.ShapeDtypeStruct(users.shape, bf16),
            jax.ShapeDtypeStruct(items.shape, f32),
            jax.ShapeDtypeStruct(items.shape, f32),
        ),
        in_specs=[any_space] * 4,
        out_specs=(any_space, vmem, vmem),
        scratch_shapes=[
            pltpu.VMEM((2, USERS, HALF), bf16),
            pltpu.VMEM((USERS, STEPS, BLOCK), bf16),
            pltpu.VMEM((STEPS, USERS, BLOCK), bf16),
            pltpu.VMEM((128 * STEPS, 128), f32),
            pltpu.VMEM((128 * STEPS, 128), f32),
            pltpu.VMEM((2, 8, R), f32),
            pltpu.VMEM((2, CHIPS, ROWS, HALF), bf16),
            pltpu.VMEM((STEPS, 2, BLOCK, HALF), bf16),
            pltpu.VMEM((USERS, BLOCK), f32),
            pltpu.VMEM((USERS, BLOCK), bf16),
            pltpu.VMEM((BLOCK, USERS), bf16),
            pltpu.VMEM((2, CHIPS, 2, 8, HALF), f32),
            pltpu.VMEM((STEPS, BLOCK, HALF), bf16),
            pltpu.VMEM((STEPS, BLOCK, HALF), bf16),
            pltpu.VMEM((STEPS, BLOCK, HALF), bf16),
            pltpu.VMEM((STEPS, CHIPS, ROWS, HALF), bf16),
            pltpu.VMEM((STEPS, 2, ROWS, HALF), f32),
            pltpu.VMEM((STEPS, 2, ROWS, HALF), f32),
            dma((5,)),
            dma((STEPS, CHIPS)),
            dma((STEPS, CHIPS)),
            dma((STEPS, CHIPS)),
            dma((STEPS, CHIPS)),
            dma((STEPS,)),
            dma((STEPS,)),
            dma((STEPS, CHIPS)),
            dma((STEPS, CHIPS)),
            dma((STEPS, 2)),
            dma((STEPS, 2)),
        ],
        compiler_params=pltpu.CompilerParams(
            collective_id=0, has_side_effects=True, vmem_limit_bytes=62 * 1024 * 1024
        ),
        cost_estimate=pl.CostEstimate(
            flops=STEPS * 6 * USERS * BLOCK * R,
            bytes_accessed=4 * 1024 * 1024,
            transcendentals=0,
        ),
    )(users, items, momentum, ratings)


def solution(mesh):
    rows = P(("stratum", "user"), None)
    return jax.shard_map(
        local,
        mesh=mesh,
        in_specs=(rows, rows, rows, P(("stratum", "user"), None, None)),
        out_specs=(rows, rows, rows),
        check_vma=False,
    )
```

```python
import functools

import jax
import jax.numpy as jnp
from jax import lax
from jax.experimental import pallas as pl
from jax.experimental.pallas import tpu as pltpu
from jax.sharding import PartitionSpec as P

R = 512
HALF = 256
STEPS = 4
USERS = 1024
BLOCK = 256
X = 4
Z = 4
CHIPS = 16
ROWS = 16
STRATA = 16
FACTOR = R**-0.5
user_rate = 1.0
item_rate = 0.04
inertia = 0.6

MESH = pl.DeviceIdType.MESH
NT = (((1,), (1,)), ((), ()))
NN = (((1,), (0,)), ((), ()))
TILE = 256


def dot(a, b, dims):
    return lax.dot_general(a, b, dims, preferred_element_type=jnp.float32)


def kernel(
    users_in,
    items_in,
    momentum_in,
    ratings_in,
    users_out,
    items_out,
    momentum_out,
    u,
    raw,
    x,
    wide0,
    wide1,
    own,
    first,
    w,
    score,
    e,
    et,
    g,
    give,
    take,
    part,
    parts,
    state,
    fresh,
    load_sem,
    ag_send,
    ag_recv,
    fw_send,
    fw_recv,
    sib_send,
    sib_recv,
    rs_send,
    rs_recv,
    st_send,
    st_recv,
):
    s = lax.axis_index("stratum")
    me = lax.axis_index("user")
    core = me % 2
    chip = me // 2
    mx, mz = chip // Z, chip % Z
    prev = (s + STRATA - 1) % STRATA
    nxt = (s + 1) % STRATA
    other = 1 - core

    def chip_at(dx, dz):
        return ((mx + dx) % X) * Z + (mz + dz) % Z

    def dev(k, c):
        return k * 2 + c

    loads = [
        pltpu.make_async_copy(items_in, own.at[0], load_sem.at[0]),
        pltpu.make_async_copy(momentum_in, own.at[1], load_sem.at[1]),
        pltpu.make_async_copy(ratings_in, raw, load_sem.at[2]),
        pltpu.make_async_copy(users_in.at[:, pl.ds(0, HALF)], u.at[0], load_sem.at[3]),
        pltpu.make_async_copy(users_in.at[:, pl.ds(HALF, HALF)], u.at[1], load_sem.at[4]),
    ]
    for copy in loads:
        copy.start()

    far = [(dx, dz) for dx in (2, 1, 3, 0) for dz in (2, 1, 3, 0)]
    far_prev = [(dx, dz) for dx in (2, 1, 3, 0) for dz in (0, 1, 3, 2)]
    barrier = pltpu.get_barrier_semaphore()

    def hello(stratum, user):
        pl.semaphore_signal(barrier, inc=1, device_id=(stratum, user), device_id_type=MESH)

    for dx, dz in far[:-1]:
        hello(s, dev(chip_at(dx, dz), core))
    hello(nxt, me)
    hello(s, dev(chip, other))
    loads[0].wait()
    loads[1].wait()
    first[core, chip] = jnp.concatenate([own[0, :, :HALF], own[0, :, HALF:]], axis=0).astype(
        jnp.bfloat16
    )
    pl.semaphore_wait(barrier, CHIPS + 1)

    def remote(src, dst, send, recv, stratum, user):
        return pltpu.make_async_remote_copy(
            src_ref=src,
            dst_ref=dst,
            send_sem=send,
            recv_sem=recv,
            device_id=(stratum, user),
            device_id_type=MESH,
        )

    def rows_of(k):
        return pl.ds(pl.multiple_of(k * ROWS, ROWS), ROWS)

    def spread(t, place):
        sends = []
        mine = place(core, chip)
        for dx, dz in far[:-1]:
            k = chip_at(dx, dz)
            sends.append(
                remote(mine, mine, ag_send.at[t, dx * Z + dz], ag_recv.at[t, chip], s, dev(k, core))
            )
            sends[-1].start()
        passed = []

        def pass_on(k, slot):
            piece = place(core, k)
            passed.append(
                remote(piece, piece, fw_send.at[t, slot], fw_recv.at[t, k], s, dev(chip, other))
            )
            passed[-1].start()

        pass_on(chip, 0)
        return sends, passed, pass_on

    def collect(t, place, pass_on):
        for slot, (dx, dz) in enumerate(far[:-1][::-1]):
            k = chip_at(dx, dz)
            piece = place(core, k)
            remote(piece, piece, ag_send.at[t, 0], ag_recv.at[t, k], s, me).wait_recv()
            pass_on(k, slot + 1)

    def collect_passed(t, place):
        for dx, dz in far[::-1]:
            k = chip_at(dx, dz)
            piece = place(other, k)
            remote(piece, piece, fw_send.at[t, 0], fw_recv.at[t, k], s, me).wait_recv()

    def finish(sends):
        for copy in sends:
            copy.wait_send()

    def place_first(c, k):
        return first.at[c, k]

    sends, passed, pass_on = spread(0, place_first)
    loads[2].wait()

    def split(i, _):
        r = pl.ds(pl.multiple_of(i * 128, 128), 128)
        for h, wide in enumerate((wide0, wide1)):
            lanes = slice(h * 128, h * 128 + 128)
            wide[...] = raw[r, :, lanes].astype(jnp.float32).reshape(128 * STEPS, 128)
        for t in range(STEPS):
            for h, wide in enumerate((wide0, wide1)):
                lanes = slice(h * 128, h * 128 + 128)
                x[t, r, lanes] = wide[pl.ds(t, 128, stride=STEPS), :].astype(jnp.bfloat16)
        return 0

    lax.fori_loop(0, USERS // 128, split, 0)
    loads[3].wait()
    loads[4].wait()

    collect(0, place_first, pass_on)
    collect_passed(0, place_first)
    finish(sends + passed)
    pieces = [first[c].astype(jnp.float32).reshape(CHIPS, 2, 8, HALF) for c in range(2)]
    for h in range(2):
        w[0, h] = (
            jnp.concatenate([pieces[0][:, h : h + 1], pieces[1][:, h : h + 1]], axis=1)
            .reshape(BLOCK, HALF)
            .astype(jnp.bfloat16)
        )

    moves = []

    def pass_state(src, t, split_rows):
        if not split_rows:
            moves.append(
                remote(src, state.at[t], st_send.at[t, 0], st_recv.at[t, 0], prev, me)
            )
            moves[-1].start()
            return
        for c in range(2):
            moves.append(
                remote(
                    src.at[:, :, pl.ds(c * HALF, HALF)] if t == 0 else src.at[:, pl.ds(c * 8, 8), :],
                    state.at[t, :, pl.ds(pl.multiple_of(core * 8, 8), 8), :],
                    st_send.at[t, c],
                    st_recv.at[t, core],
                    prev,
                    dev(chip, c),
                )
            )
            moves[-1].start()

    for t in range(STEPS):
        last = t == STEPS - 1

        def place(c, k, t=t):
            return w.at[t, c, rows_of(k), :]

        tiles = [pl.ds(i * TILE, TILE) for i in range(USERS // TILE)]
        if t == 0:
            pass_state(own, 0, True)
            for r in tiles:
                score[r, :] = dot(u[core, r, :], w[t, core], NT)
        else:
            for r in tiles:
                score[r, :] = dot(u[core, r, :], w[t, core], NT)
            collect_passed(t, place)
            pass_state(fresh.at[t - 1], t, last)
            finish(sends + passed)
        for r in tiles:
            total = score[r, :] + dot(u[other, r, :], w[t, other], NT)
            tile = x[t, r, :].astype(jnp.float32)
            resid = jnp.where(tile != 0, total * FACTOR - tile, 0.0).astype(jnp.bfloat16)
            e[r, :] = resid
            et[:, r] = resid.T
        if last:
            for h in range(2):
                g[h] = dot(et[...], u[h], NN).reshape(CHIPS, 2, 8, HALF)

            def piece_for(c):
                both = [g[h, :, pl.ds(c, 1)] for h in range(2)]
                return jnp.concatenate(both, axis=1).reshape(BLOCK, HALF)

            give[t] = piece_for(other).astype(jnp.bfloat16)
        else:
            give[t] = dot(et[...], u[other], NN).astype(jnp.bfloat16)
        swap = remote(
            give.at[t], take.at[t], sib_send.at[t], sib_recv.at[t], s, dev(chip, other)
        )
        swap.start()
        if not last:
            g[0] = dot(et[...], u[core], NN).reshape(CHIPS, 2, 8, HALF)
        for h in range(2):
            for r in tiles:
                change = dot(e[r, :], w[t, h], NN)
                moved = (u[h, r, :].astype(jnp.float32) - user_rate * FACTOR * change).astype(
                    jnp.bfloat16
                )
                if last:
                    users_out[r, h * HALF : h * HALF + HALF] = moved
                else:
                    u[h, r, :] = moved
        swap.wait_recv()
        mine = piece_for(core) if last else g[0].reshape(BLOCK, HALF)
        part[t] = (mine + take[t].astype(jnp.float32)).astype(jnp.bfloat16)
        gives = []
        for dx, dz in far_prev:
            k = chip_at(dx, dz)
            gives.append(
                remote(
                    part.at[t, rows_of(k), :],
                    parts.at[t, chip],
                    rs_send.at[t, dx * Z + dz],
                    rs_recv.at[t, chip],
                    prev,
                    dev(k, core),
                )
            )
            gives[-1].start()
        if t == 0 or last:
            for c in range(2):
                remote(
                    own.at[:, :, pl.ds(c * HALF, HALF)],
                    state.at[t, :, pl.ds(c * 8, 8), :],
                    st_send.at[t, c],
                    st_recv.at[t, c],
                    s,
                    me,
                ).wait_recv()
        else:
            remote(
                fresh.at[t], state.at[t], st_send.at[t, 0], st_recv.at[t, 0], s, me
            ).wait_recv()
        for dx, dz in far_prev[::-1]:
            k = chip_at(dx, dz)
            remote(
                part.at[t, rows_of(k), :], parts.at[t, k], rs_send.at[t, 0], rs_recv.at[t, k], s, me
            ).wait_recv()
        grads = jnp.sum(parts[t].astype(jnp.float32), axis=0)
        momentum = inertia * state[t, 1] + FACTOR * grads
        items = state[t, 0] - item_rate * momentum
        if last:
            for h in range(2):
                items_out[:, h * HALF : h * HALF + HALF] = items[h * 8 : h * 8 + 8]
                momentum_out[:, h * HALF : h * HALF + HALF] = momentum[h * 8 : h * 8 + 8]
        else:
            w[t + 1, core, rows_of(chip), :] = items.astype(jnp.bfloat16)

            def place(c, k, t=t + 1):
                return w.at[t, c, rows_of(k), :]

            sends, passed, pass_on = spread(t + 1, place)
            fresh[t, 0] = items
            fresh[t, 1] = momentum
            collect(t + 1, place, pass_on)
        moves += [*gives, swap]
    finish(moves)


def write_out(users, items, momentum, users_out, items_out, momentum_out, sem):
    copies = [
        pltpu.make_async_copy(users, users_out, sem.at[0]),
        pltpu.make_async_copy(items, items_out, sem.at[1]),
        pltpu.make_async_copy(momentum, momentum_out, sem.at[2]),
    ]
    for copy in copies:
        copy.start()
    for copy in copies:
        copy.wait()


def local(users, items, momentum, ratings):
    bf16, f32 = jnp.bfloat16, jnp.float32
    any_space = pl.BlockSpec(memory_space=pl.ANY)
    vmem = pl.BlockSpec(memory_space=pltpu.VMEM)
    dma = pltpu.SemaphoreType.DMA
    inputs = [
        pltpu.with_memory_space_constraint(a, pltpu.HBM) for a in (users, items, momentum, ratings)
    ]
    outs = pl.pallas_call(
        kernel,
        out_shape=(
            pltpu.VMEM(users.shape, bf16),
            pltpu.VMEM(items.shape, f32),
            pltpu.VMEM(items.shape, f32),
        ),
        in_specs=[any_space] * 4,
        out_specs=(vmem, vmem, vmem),
        scratch_shapes=[
            pltpu.VMEM((2, USERS, HALF), bf16),
            pltpu.VMEM((USERS, STEPS, BLOCK), bf16),
            pltpu.VMEM((STEPS, USERS, BLOCK), bf16),
            pltpu.VMEM((128 * STEPS, 128), f32),
            pltpu.VMEM((128 * STEPS, 128), f32),
            pltpu.VMEM((2, 8, R), f32),
            pltpu.VMEM((2, CHIPS, ROWS, HALF), bf16),
            pltpu.VMEM((STEPS, 2, BLOCK, HALF), bf16),
            pltpu.VMEM((USERS, BLOCK), f32),
            pltpu.VMEM((USERS, BLOCK), bf16),
            pltpu.VMEM((BLOCK, USERS), bf16),
            pltpu.VMEM((2, CHIPS, 2, 8, HALF), f32),
            pltpu.VMEM((STEPS, BLOCK, HALF), bf16),
            pltpu.VMEM((STEPS, BLOCK, HALF), bf16),
            pltpu.VMEM((STEPS, BLOCK, HALF), bf16),
            pltpu.VMEM((STEPS, CHIPS, ROWS, HALF), bf16),
            pltpu.VMEM((STEPS, 2, ROWS, HALF), f32),
            pltpu.VMEM((STEPS, 2, ROWS, HALF), f32),
            dma((5,)),
            dma((STEPS, CHIPS)),
            dma((STEPS, CHIPS)),
            dma((STEPS, CHIPS)),
            dma((STEPS, CHIPS)),
            dma((STEPS,)),
            dma((STEPS,)),
            dma((STEPS, CHIPS)),
            dma((STEPS, CHIPS)),
            dma((STEPS, 2)),
            dma((STEPS, 2)),
        ],
        compiler_params=pltpu.CompilerParams(
            collective_id=0, has_side_effects=True, vmem_limit_bytes=48 * 1024 * 1024
        ),
        cost_estimate=pl.CostEstimate(
            flops=STEPS * 6 * USERS * BLOCK * R,
            bytes_accessed=4 * 1024 * 1024,
            transcendentals=0,
        ),
    )(*inputs)
    outs = [pltpu.with_memory_space_constraint(a, pltpu.VMEM) for a in outs]
    return pl.pallas_call(
        write_out,
        out_shape=(
            jax.ShapeDtypeStruct(users.shape, bf16),
            jax.ShapeDtypeStruct(items.shape, f32),
            jax.ShapeDtypeStruct(items.shape, f32),
        ),
        in_specs=[any_space] * 3,
        out_specs=(any_space,) * 3,
        scratch_shapes=[dma((3,))],
    )(*outs)


def solution(mesh):
    rows = P(("stratum", "user"), None)
    return jax.shard_map(
        local,
        mesh=mesh,
        in_specs=(rows, rows, rows, P(("stratum", "user"), None, None)),
        out_specs=(rows, rows, rows),
        check_vma=False,
    )
```

```python
import functools

import jax
import jax.numpy as jnp
from jax import lax
from jax.experimental import pallas as pl
from jax.experimental.pallas import tpu as pltpu
from jax.sharding import PartitionSpec as P

R = 512
HALF = 256
STEPS = 4
USERS = 1024
BLOCK = 256
X = 4
Z = 4
CHIPS = 16
ROWS = 16
STRATA = 16
FACTOR = R**-0.5
user_rate = 1.0
item_rate = 0.04
inertia = 0.6

MESH = pl.DeviceIdType.MESH
NT = (((1,), (1,)), ((), ()))
NN = (((1,), (0,)), ((), ()))
TILE = 256


def dot(a, b, dims):
    return lax.dot_general(a, b, dims, preferred_element_type=jnp.float32)


def kernel(
    users_in,
    items_in,
    momentum_in,
    ratings_in,
    users_out,
    items_out,
    momentum_out,
    u,
    raw,
    x,
    wide0,
    wide1,
    own,
    first,
    w,
    score,
    e,
    et,
    g,
    give,
    take,
    part,
    along_x,
    line,
    parts,
    state,
    fresh,
    load_sem,
    ag_send,
    ag_recv,
    fw_send,
    fw_recv,
    sib_send,
    sib_recv,
    x_send,
    x_recv,
    rs_send,
    rs_recv,
    st_send,
    st_recv,
):
    s = lax.axis_index("stratum")
    me = lax.axis_index("user")
    core = me % 2
    chip = me // 2
    mx, mz = chip // Z, chip % Z
    prev = (s + STRATA - 1) % STRATA
    nxt = (s + 1) % STRATA
    other = 1 - core

    def chip_at(dx, dz):
        return ((mx + dx) % X) * Z + (mz + dz) % Z

    def dev(k, c):
        return k * 2 + c

    loads = [
        pltpu.make_async_copy(items_in, own.at[0], load_sem.at[0]),
        pltpu.make_async_copy(momentum_in, own.at[1], load_sem.at[1]),
        pltpu.make_async_copy(ratings_in, raw, load_sem.at[2]),
        pltpu.make_async_copy(users_in.at[:, pl.ds(0, HALF)], u.at[0], load_sem.at[3]),
        pltpu.make_async_copy(users_in.at[:, pl.ds(HALF, HALF)], u.at[1], load_sem.at[4]),
    ]

    far = [(dx, dz) for dx in (2, 1, 3, 0) for dz in (2, 1, 3, 0)]
    barrier = pltpu.get_barrier_semaphore()

    def hello(stratum, user):
        pl.semaphore_signal(barrier, inc=1, device_id=(stratum, user), device_id_type=MESH)

    hello(nxt, me)
    for dx, dz in far[:-1]:
        hello(s, dev(chip_at(dx, dz), core))
    hello(s, dev(chip, other))
    for copy in loads:
        copy.start()
    loads[0].wait()
    loads[1].wait()
    first[core, chip] = jnp.concatenate([own[0, :, :HALF], own[0, :, HALF:]], axis=0).astype(
        jnp.bfloat16
    )
    pl.semaphore_wait(barrier, CHIPS + 1)

    def remote(src, dst, send, recv, stratum, user):
        return pltpu.make_async_remote_copy(
            src_ref=src,
            dst_ref=dst,
            send_sem=send,
            recv_sem=recv,
            device_id=(stratum, user),
            device_id_type=MESH,
        )

    def lines_of(k):
        return pl.ds(pl.multiple_of(k * (Z * ROWS), Z * ROWS), Z * ROWS)

    def rows_of(k):
        return pl.ds(pl.multiple_of(k * ROWS, ROWS), ROWS)

    def spread(t, place):
        sends = []
        mine = place(core, chip)
        for dx, dz in far[:-1]:
            k = chip_at(dx, dz)
            sends.append(
                remote(mine, mine, ag_send.at[t, dx * Z + dz], ag_recv.at[t, chip], s, dev(k, core))
            )
            sends[-1].start()
        passed = []

        def pass_on(k, slot):
            piece = place(core, k)
            passed.append(
                remote(piece, piece, fw_send.at[t, slot], fw_recv.at[t, k], s, dev(chip, other))
            )
            passed[-1].start()

        pass_on(chip, 0)
        return sends, passed, pass_on

    def collect(t, place, pass_on):
        for slot, (dx, dz) in enumerate(far[:-1][::-1]):
            k = chip_at(dx, dz)
            piece = place(core, k)
            remote(piece, piece, ag_send.at[t, 0], ag_recv.at[t, k], s, me).wait_recv()
            pass_on(k, slot + 1)

    def collect_passed(t, place):
        for dx, dz in far[::-1]:
            k = chip_at(dx, dz)
            piece = place(other, k)
            remote(piece, piece, fw_send.at[t, 0], fw_recv.at[t, k], s, me).wait_recv()

    def finish(sends):
        for copy in sends:
            copy.wait_send()

    def place_first(c, k):
        return first.at[c, k]

    sends, passed, pass_on = spread(0, place_first)
    loads[2].wait()

    def split(i, _):
        r = pl.ds(pl.multiple_of(i * 128, 128), 128)
        for h, wide in enumerate((wide0, wide1)):
            lanes = slice(h * 128, h * 128 + 128)
            wide[...] = raw[r, :, lanes].astype(jnp.float32).reshape(128 * STEPS, 128)
        for t in range(STEPS):
            for h, wide in enumerate((wide0, wide1)):
                lanes = slice(h * 128, h * 128 + 128)
                x[t, r, lanes] = wide[pl.ds(t, 128, stride=STEPS), :].astype(jnp.bfloat16)
        return 0

    lax.fori_loop(0, USERS // 128, split, 0)
    loads[3].wait()
    loads[4].wait()

    collect(0, place_first, pass_on)
    collect_passed(0, place_first)
    finish(sends + passed)
    pieces = [first[c].astype(jnp.float32).reshape(CHIPS, 2, 8, HALF) for c in range(2)]
    for h in range(2):
        w[0, h] = (
            jnp.concatenate([pieces[0][:, h : h + 1], pieces[1][:, h : h + 1]], axis=1)
            .reshape(BLOCK, HALF)
            .astype(jnp.bfloat16)
        )

    moves = []

    def pass_state(src, t, split_rows):
        if not split_rows:
            moves.append(
                remote(src, state.at[t], st_send.at[t, 0], st_recv.at[t, 0], prev, me)
            )
            moves[-1].start()
            return
        for c in range(2):
            moves.append(
                remote(
                    src.at[:, :, pl.ds(c * HALF, HALF)] if t == 0 else src.at[:, pl.ds(c * 8, 8), :],
                    state.at[t, :, pl.ds(pl.multiple_of(core * 8, 8), 8), :],
                    st_send.at[t, c],
                    st_recv.at[t, core],
                    prev,
                    dev(chip, c),
                )
            )
            moves[-1].start()

    for t in range(STEPS):
        last = t == STEPS - 1

        def place(c, k, t=t):
            return w.at[t, c, rows_of(k), :]

        tiles = [pl.ds(i * TILE, TILE) for i in range(USERS // TILE)]
        if t == 0:
            pass_state(own, 0, True)
            for r in tiles:
                score[r, :] = dot(u[core, r, :], w[t, core], NT)
        else:
            for r in tiles:
                score[r, :] = dot(u[core, r, :], w[t, core], NT)
            collect_passed(t, place)
            pass_state(fresh.at[t - 1], t, last)
            finish(sends + passed)
        for r in tiles:
            total = score[r, :] + dot(u[other, r, :], w[t, other], NT)
            tile = x[t, r, :].astype(jnp.float32)
            resid = jnp.where(tile != 0, total * FACTOR - tile, 0.0).astype(jnp.bfloat16)
            e[r, :] = resid
            et[:, r] = resid.T
        if last:
            for h in range(2):
                g[h] = dot(et[...], u[h], NN).reshape(CHIPS, 2, 8, HALF)

            def piece_for(c):
                both = [g[h, :, pl.ds(c, 1)] for h in range(2)]
                return jnp.concatenate(both, axis=1).reshape(BLOCK, HALF)

            give[t] = piece_for(other).astype(jnp.bfloat16)
        else:
            give[t] = dot(et[...], u[other], NN).astype(jnp.bfloat16)
        swap = remote(
            give.at[t], take.at[t], sib_send.at[t], sib_recv.at[t], s, dev(chip, other)
        )
        swap.start()
        if not last:
            g[0] = dot(et[...], u[core], NN).reshape(CHIPS, 2, 8, HALF)
        for h in range(2):
            for r in tiles:
                change = dot(e[r, :], w[t, h], NN)
                moved = (u[h, r, :].astype(jnp.float32) - user_rate * FACTOR * change).astype(
                    jnp.bfloat16
                )
                if last:
                    users_out[r, h * HALF : h * HALF + HALF] = moved
                else:
                    u[h, r, :] = moved
        swap.wait_recv()
        mine = piece_for(core) if last else g[0].reshape(BLOCK, HALF)
        part[t] = (mine + take[t].astype(jnp.float32)).astype(jnp.bfloat16)
        gives = []
        for dx in (2, 1, 3):
            x_of = (mx + dx) % X
            gives.append(
                remote(
                    part.at[t, lines_of(x_of), :],
                    along_x.at[t, dx - 1],
                    x_send.at[t, dx - 1],
                    x_recv.at[t, dx - 1],
                    s,
                    dev(x_of * Z + mz, core),
                )
            )
            gives[-1].start()
        total = part[t, lines_of(mx), :].astype(jnp.float32)
        for i in (1, 2, 0):
            gives[(2, 1, 3).index(i + 1)].wait_recv()
            total += along_x[t, i].astype(jnp.float32)
        line[t] = total.astype(jnp.bfloat16)
        for dz in (0, 1, 3, 2):
            z_of = (mz + dz) % Z
            gives.append(
                remote(
                    line.at[t, rows_of(z_of), :],
                    parts.at[t, mz],
                    rs_send.at[t, dz],
                    rs_recv.at[t, mz],
                    prev,
                    dev(mx * Z + z_of, core),
                )
            )
            gives[-1].start()
        if t == 0 or last:
            for c in range(2):
                remote(
                    own.at[:, :, pl.ds(c * HALF, HALF)],
                    state.at[t, :, pl.ds(c * 8, 8), :],
                    st_send.at[t, c],
                    st_recv.at[t, c],
                    s,
                    me,
                ).wait_recv()
        else:
            remote(
                fresh.at[t], state.at[t], st_send.at[t, 0], st_recv.at[t, 0], s, me
            ).wait_recv()
        for z_of in range(Z):
            remote(
                line.at[t, rows_of(0), :],
                parts.at[t, z_of],
                rs_send.at[t, 0],
                rs_recv.at[t, z_of],
                s,
                me,
            ).wait_recv()
        grads = jnp.sum(parts[t].astype(jnp.float32), axis=0)
        momentum = inertia * state[t, 1] + FACTOR * grads
        items = state[t, 0] - item_rate * momentum
        if last:
            for h in range(2):
                items_out[:, h * HALF : h * HALF + HALF] = items[h * 8 : h * 8 + 8]
                momentum_out[:, h * HALF : h * HALF + HALF] = momentum[h * 8 : h * 8 + 8]
        else:
            w[t + 1, core, rows_of(chip), :] = items.astype(jnp.bfloat16)

            def place(c, k, t=t + 1):
                return w.at[t, c, rows_of(k), :]

            sends, passed, pass_on = spread(t + 1, place)
            fresh[t, 0] = items
            fresh[t, 1] = momentum
            collect(t + 1, place, pass_on)
        moves += [*gives, swap]
    finish(moves)


def write_out(users, items, momentum, users_out, items_out, momentum_out, sem):
    copies = [
        pltpu.make_async_copy(users, users_out, sem.at[0]),
        pltpu.make_async_copy(items, items_out, sem.at[1]),
        pltpu.make_async_copy(momentum, momentum_out, sem.at[2]),
    ]
    for copy in copies:
        copy.start()
    for copy in copies:
        copy.wait()


def local(users, items, momentum, ratings):
    bf16, f32 = jnp.bfloat16, jnp.float32
    any_space = pl.BlockSpec(memory_space=pl.ANY)
    vmem = pl.BlockSpec(memory_space=pltpu.VMEM)
    dma = pltpu.SemaphoreType.DMA
    inputs = [
        pltpu.with_memory_space_constraint(a, pltpu.HBM) for a in (users, items, momentum, ratings)
    ]
    outs = pl.pallas_call(
        kernel,
        out_shape=(
            pltpu.VMEM(users.shape, bf16),
            pltpu.VMEM(items.shape, f32),
            pltpu.VMEM(items.shape, f32),
        ),
        in_specs=[any_space] * 4,
        out_specs=(vmem, vmem, vmem),
        scratch_shapes=[
            pltpu.VMEM((2, USERS, HALF), bf16),
            pltpu.VMEM((USERS, STEPS, BLOCK), bf16),
            pltpu.VMEM((STEPS, USERS, BLOCK), bf16),
            pltpu.VMEM((128 * STEPS, 128), f32),
            pltpu.VMEM((128 * STEPS, 128), f32),
            pltpu.VMEM((2, 8, R), f32),
            pltpu.VMEM((2, CHIPS, ROWS, HALF), bf16),
            pltpu.VMEM((STEPS, 2, BLOCK, HALF), bf16),
            pltpu.VMEM((USERS, BLOCK), f32),
            pltpu.VMEM((USERS, BLOCK), bf16),
            pltpu.VMEM((BLOCK, USERS), bf16),
            pltpu.VMEM((2, CHIPS, 2, 8, HALF), f32),
            pltpu.VMEM((STEPS, BLOCK, HALF), bf16),
            pltpu.VMEM((STEPS, BLOCK, HALF), bf16),
            pltpu.VMEM((STEPS, BLOCK, HALF), bf16),
            pltpu.VMEM((STEPS, X - 1, Z * ROWS, HALF), bf16),
            pltpu.VMEM((STEPS, Z * ROWS, HALF), bf16),
            pltpu.VMEM((STEPS, Z, ROWS, HALF), bf16),
            pltpu.VMEM((STEPS, 2, ROWS, HALF), f32),
            pltpu.VMEM((STEPS, 2, ROWS, HALF), f32),
            dma((5,)),
            dma((STEPS, CHIPS)),
            dma((STEPS, CHIPS)),
            dma((STEPS, CHIPS)),
            dma((STEPS, CHIPS)),
            dma((STEPS,)),
            dma((STEPS,)),
            dma((STEPS, X - 1)),
            dma((STEPS, X - 1)),
            dma((STEPS, Z)),
            dma((STEPS, Z)),
            dma((STEPS, 2)),
            dma((STEPS, 2)),
        ],
        compiler_params=pltpu.CompilerParams(
            collective_id=0, has_side_effects=True, vmem_limit_bytes=48 * 1024 * 1024
        ),
        cost_estimate=pl.CostEstimate(
            flops=STEPS * 6 * USERS * BLOCK * R,
            bytes_accessed=4 * 1024 * 1024,
            transcendentals=0,
        ),
    )(*inputs)
    outs = [pltpu.with_memory_space_constraint(a, pltpu.VMEM) for a in outs]
    return pl.pallas_call(
        write_out,
        out_shape=(
            jax.ShapeDtypeStruct(users.shape, bf16),
            jax.ShapeDtypeStruct(items.shape, f32),
            jax.ShapeDtypeStruct(items.shape, f32),
        ),
        in_specs=[any_space] * 3,
        out_specs=(any_space,) * 3,
        scratch_shapes=[dma((3,))],
    )(*outs)


def solution(mesh):
    rows = P(("stratum", "user"), None)
    return jax.shard_map(
        local,
        mesh=mesh,
        in_specs=(rows, rows, rows, P(("stratum", "user"), None, None)),
        out_specs=(rows, rows, rows),
        check_vma=False,
    )
```

```python
import functools

import jax
import jax.numpy as jnp
from jax import lax
from jax.experimental import pallas as pl
from jax.experimental.pallas import tpu as pltpu
from jax.sharding import PartitionSpec as P

R = 512
HALF = 256
STEPS = 4
USERS = 1024
BLOCK = 256
X = 4
Z = 4
CHIPS = 16
ROWS = 16
STRATA = 16
FACTOR = R**-0.5
user_rate = 1.0
item_rate = 0.04
inertia = 0.6

MESH = pl.DeviceIdType.MESH
NT = (((1,), (1,)), ((), ()))
NN = (((1,), (0,)), ((), ()))
TILE = 256


def dot(a, b, dims):
    return lax.dot_general(a, b, dims, preferred_element_type=jnp.float32)


def kernel(
    users_in,
    items_in,
    momentum_in,
    ratings_in,
    users_out,
    items_out,
    momentum_out,
    u,
    raw,
    x,
    wide0,
    wide1,
    own,
    first,
    w,
    score,
    e,
    et,
    g,
    give,
    take,
    part,
    along_x,
    line,
    parts,
    state,
    fresh,
    load_sem,
    ag_send,
    ag_recv,
    fw_send,
    fw_recv,
    sib_send,
    sib_recv,
    x_send,
    x_recv,
    rs_send,
    rs_recv,
    st_send,
    st_recv,
):
    s = lax.axis_index("stratum")
    me = lax.axis_index("user")
    core = me % 2
    chip = me // 2
    mx, mz = chip // Z, chip % Z
    prev = (s + STRATA - 1) % STRATA
    nxt = (s + 1) % STRATA
    other = 1 - core

    def chip_at(dx, dz):
        return ((mx + dx) % X) * Z + (mz + dz) % Z

    def dev(k, c):
        return k * 2 + c

    loads = [
        pltpu.make_async_copy(items_in, own.at[0], load_sem.at[0]),
        pltpu.make_async_copy(momentum_in, own.at[1], load_sem.at[1]),
        pltpu.make_async_copy(ratings_in, raw, load_sem.at[2]),
        pltpu.make_async_copy(users_in.at[:, pl.ds(0, HALF)], u.at[0], load_sem.at[3]),
        pltpu.make_async_copy(users_in.at[:, pl.ds(HALF, HALF)], u.at[1], load_sem.at[4]),
    ]

    loads[0].start()
    loads[1].start()
    far = [(dx, dz) for dx in (2, 1, 3, 0) for dz in (2, 1, 3, 0)]
    barrier = pltpu.get_barrier_semaphore()

    def hello(stratum, user):
        pl.semaphore_signal(barrier, inc=1, device_id=(stratum, user), device_id_type=MESH)

    hello(nxt, me)
    for dx, dz in far[:-1]:
        hello(s, dev(chip_at(dx, dz), core))
    hello(s, dev(chip, other))
    for copy in loads[2:]:
        copy.start()
    loads[0].wait()
    loads[1].wait()
    first[core, chip] = jnp.concatenate([own[0, :, :HALF], own[0, :, HALF:]], axis=0).astype(
        jnp.bfloat16
    )
    pl.semaphore_wait(barrier, CHIPS + 1)

    def remote(src, dst, send, recv, stratum, user):
        return pltpu.make_async_remote_copy(
            src_ref=src,
            dst_ref=dst,
            send_sem=send,
            recv_sem=recv,
            device_id=(stratum, user),
            device_id_type=MESH,
        )

    def lines_of(k):
        return pl.ds(pl.multiple_of(k * (Z * ROWS), Z * ROWS), Z * ROWS)

    def rows_of(k):
        return pl.ds(pl.multiple_of(k * ROWS, ROWS), ROWS)

    def spread(t, place):
        sends = []
        mine = place(core, chip)
        for dx, dz in far[:-1]:
            k = chip_at(dx, dz)
            sends.append(
                remote(mine, mine, ag_send.at[t, dx * Z + dz], ag_recv.at[t, chip], s, dev(k, core))
            )
            sends[-1].start()
        passed = []

        def pass_on(k, slot):
            piece = place(core, k)
            passed.append(
                remote(piece, piece, fw_send.at[t, slot], fw_recv.at[t, k], s, dev(chip, other))
            )
            passed[-1].start()

        pass_on(chip, 0)
        return sends, passed, pass_on

    def collect(t, place, pass_on):
        for slot, (dx, dz) in enumerate(far[:-1][::-1]):
            k = chip_at(dx, dz)
            piece = place(core, k)
            remote(piece, piece, ag_send.at[t, 0], ag_recv.at[t, k], s, me).wait_recv()
            pass_on(k, slot + 1)

    def collect_passed(t, place):
        for dx, dz in far[::-1]:
            k = chip_at(dx, dz)
            piece = place(other, k)
            remote(piece, piece, fw_send.at[t, 0], fw_recv.at[t, k], s, me).wait_recv()

    def finish(sends):
        for copy in sends:
            copy.wait_send()

    def place_first(c, k):
        return first.at[c, k]

    sends, passed, pass_on = spread(0, place_first)
    loads[2].wait()

    def split(i, _):
        r = pl.ds(pl.multiple_of(i * 128, 128), 128)
        for h, wide in enumerate((wide0, wide1)):
            lanes = slice(h * 128, h * 128 + 128)
            wide[...] = raw[r, :, lanes].astype(jnp.float32).reshape(128 * STEPS, 128)
        for t in range(STEPS):
            for h, wide in enumerate((wide0, wide1)):
                lanes = slice(h * 128, h * 128 + 128)
                x[t, r, lanes] = wide[pl.ds(t, 128, stride=STEPS), :].astype(jnp.bfloat16)
        return 0

    lax.fori_loop(0, USERS // 128, split, 0)
    loads[3].wait()
    loads[4].wait()

    collect(0, place_first, pass_on)
    collect_passed(0, place_first)
    finish(sends + passed)
    pieces = [first[c].astype(jnp.float32).reshape(CHIPS, 2, 8, HALF) for c in range(2)]
    for h in range(2):
        w[0, h] = (
            jnp.concatenate([pieces[0][:, h : h + 1], pieces[1][:, h : h + 1]], axis=1)
            .reshape(BLOCK, HALF)
            .astype(jnp.bfloat16)
        )

    moves = []

    def pass_state(src, t, split_rows):
        if not split_rows:
            moves.append(
                remote(src, state.at[t], st_send.at[t, 0], st_recv.at[t, 0], prev, me)
            )
            moves[-1].start()
            return
        for c in range(2):
            moves.append(
                remote(
                    src.at[:, :, pl.ds(c * HALF, HALF)] if t == 0 else src.at[:, pl.ds(c * 8, 8), :],
                    state.at[t, :, pl.ds(pl.multiple_of(core * 8, 8), 8), :],
                    st_send.at[t, c],
                    st_recv.at[t, core],
                    prev,
                    dev(chip, c),
                )
            )
            moves[-1].start()

    for t in range(STEPS):
        last = t == STEPS - 1

        def place(c, k, t=t):
            return w.at[t, c, rows_of(k), :]

        tiles = [pl.ds(i * TILE, TILE) for i in range(USERS // TILE)]
        if t == 0:
            pass_state(own, 0, True)
            for r in tiles:
                score[r, :] = dot(u[core, r, :], w[t, core], NT)
        else:
            for r in tiles:
                score[r, :] = dot(u[core, r, :], w[t, core], NT)
            collect_passed(t, place)
            pass_state(fresh.at[t - 1], t, last)
            finish(sends + passed)
        for r in tiles:
            total = score[r, :] + dot(u[other, r, :], w[t, other], NT)
            tile = x[t, r, :].astype(jnp.float32)
            resid = jnp.where(tile != 0, total * FACTOR - tile, 0.0).astype(jnp.bfloat16)
            e[r, :] = resid
            et[:, r] = resid.T
        if last:
            for h in range(2):
                g[h] = dot(et[...], u[h], NN).reshape(CHIPS, 2, 8, HALF)

            def piece_for(c):
                both = [g[h, :, pl.ds(c, 1)] for h in range(2)]
                return jnp.concatenate(both, axis=1).reshape(BLOCK, HALF)

            give[t] = piece_for(other).astype(jnp.bfloat16)
        else:
            give[t] = dot(et[...], u[other], NN).astype(jnp.bfloat16)
        swaps = {}
        for dx in (2, 1, 3, 0):
            lines = lines_of((mx + dx) % X)
            swaps[dx] = remote(
                give.at[t, lines, :],
                take.at[t, lines, :],
                sib_send.at[t, dx],
                sib_recv.at[t, dx],
                s,
                dev(chip, other),
            )
            swaps[dx].start()
        if not last:
            g[0] = dot(et[...], u[core], NN).reshape(CHIPS, 2, 8, HALF)
        for h in range(2):
            for r in tiles:
                change = dot(e[r, :], w[t, h], NN)
                moved = (u[h, r, :].astype(jnp.float32) - user_rate * FACTOR * change).astype(
                    jnp.bfloat16
                )
                if last:
                    users_out[r, h * HALF : h * HALF + HALF] = moved
                else:
                    u[h, r, :] = moved

        def chip_sum(dx, t=t, last=last, swaps=swaps):
            x_of = (mx + dx) % X
            four = pl.ds(x_of * Z, Z)
            if last:
                both = [g[h, four, pl.ds(core, 1)] for h in range(2)]
                mine = jnp.concatenate(both, axis=1)
            else:
                mine = g[0, four]
            swaps[dx].wait_recv()
            return mine.reshape(Z * ROWS, HALF) + take[t, lines_of(x_of), :].astype(jnp.float32)

        gives = []
        for dx in (2, 1, 3):
            x_of = (mx + dx) % X
            part[t, lines_of(x_of), :] = chip_sum(dx).astype(jnp.bfloat16)
            gives.append(
                remote(
                    part.at[t, lines_of(x_of), :],
                    along_x.at[t, dx - 1],
                    x_send.at[t, dx - 1],
                    x_recv.at[t, dx - 1],
                    s,
                    dev(x_of * Z + mz, core),
                )
            )
            gives[-1].start()
        total = chip_sum(0)
        for i in (1, 2, 0):
            gives[(2, 1, 3).index(i + 1)].wait_recv()
            total += along_x[t, i].astype(jnp.float32)
        line[t] = total.astype(jnp.bfloat16)
        for dz in (0, 1, 3, 2):
            z_of = (mz + dz) % Z
            gives.append(
                remote(
                    line.at[t, rows_of(z_of), :],
                    parts.at[t, mz],
                    rs_send.at[t, dz],
                    rs_recv.at[t, mz],
                    prev,
                    dev(mx * Z + z_of, core),
                )
            )
            gives[-1].start()
        if t == 0 or last:
            for c in range(2):
                remote(
                    own.at[:, :, pl.ds(c * HALF, HALF)],
                    state.at[t, :, pl.ds(c * 8, 8), :],
                    st_send.at[t, c],
                    st_recv.at[t, c],
                    s,
                    me,
                ).wait_recv()
        else:
            remote(
                fresh.at[t], state.at[t], st_send.at[t, 0], st_recv.at[t, 0], s, me
            ).wait_recv()
        for z_of in range(Z):
            remote(
                line.at[t, rows_of(0), :],
                parts.at[t, z_of],
                rs_send.at[t, 0],
                rs_recv.at[t, z_of],
                s,
                me,
            ).wait_recv()
        grads = jnp.sum(parts[t].astype(jnp.float32), axis=0)
        momentum = inertia * state[t, 1] + FACTOR * grads
        items = state[t, 0] - item_rate * momentum
        if last:
            for h in range(2):
                items_out[:, h * HALF : h * HALF + HALF] = items[h * 8 : h * 8 + 8]
                momentum_out[:, h * HALF : h * HALF + HALF] = momentum[h * 8 : h * 8 + 8]
        else:
            w[t + 1, core, rows_of(chip), :] = items.astype(jnp.bfloat16)

            def place(c, k, t=t + 1):
                return w.at[t, c, rows_of(k), :]

            sends, passed, pass_on = spread(t + 1, place)
            fresh[t, 0] = items
            fresh[t, 1] = momentum
            collect(t + 1, place, pass_on)
        moves += [*gives, *swaps.values()]
    finish(moves)


def write_out(users, items, momentum, users_out, items_out, momentum_out, sem):
    copies = [
        pltpu.make_async_copy(users, users_out, sem.at[0]),
        pltpu.make_async_copy(items, items_out, sem.at[1]),
        pltpu.make_async_copy(momentum, momentum_out, sem.at[2]),
    ]
    for copy in copies:
        copy.start()
    for copy in copies:
        copy.wait()


def local(users, items, momentum, ratings):
    bf16, f32 = jnp.bfloat16, jnp.float32
    any_space = pl.BlockSpec(memory_space=pl.ANY)
    vmem = pl.BlockSpec(memory_space=pltpu.VMEM)
    dma = pltpu.SemaphoreType.DMA
    inputs = [
        pltpu.with_memory_space_constraint(a, pltpu.HBM) for a in (users, items, momentum, ratings)
    ]
    outs = pl.pallas_call(
        kernel,
        out_shape=(
            pltpu.VMEM(users.shape, bf16),
            pltpu.VMEM(items.shape, f32),
            pltpu.VMEM(items.shape, f32),
        ),
        in_specs=[any_space] * 4,
        out_specs=(vmem, vmem, vmem),
        scratch_shapes=[
            pltpu.VMEM((2, USERS, HALF), bf16),
            pltpu.VMEM((USERS, STEPS, BLOCK), bf16),
            pltpu.VMEM((STEPS, USERS, BLOCK), bf16),
            pltpu.VMEM((128 * STEPS, 128), f32),
            pltpu.VMEM((128 * STEPS, 128), f32),
            pltpu.VMEM((2, 8, R), f32),
            pltpu.VMEM((2, CHIPS, ROWS, HALF), bf16),
            pltpu.VMEM((STEPS, 2, BLOCK, HALF), bf16),
            pltpu.VMEM((USERS, BLOCK), f32),
            pltpu.VMEM((USERS, BLOCK), bf16),
            pltpu.VMEM((BLOCK, USERS), bf16),
            pltpu.VMEM((2, CHIPS, 2, 8, HALF), f32),
            pltpu.VMEM((STEPS, BLOCK, HALF), bf16),
            pltpu.VMEM((STEPS, BLOCK, HALF), bf16),
            pltpu.VMEM((STEPS, BLOCK, HALF), bf16),
            pltpu.VMEM((STEPS, X - 1, Z * ROWS, HALF), bf16),
            pltpu.VMEM((STEPS, Z * ROWS, HALF), bf16),
            pltpu.VMEM((STEPS, Z, ROWS, HALF), bf16),
            pltpu.VMEM((STEPS, 2, ROWS, HALF), f32),
            pltpu.VMEM((STEPS, 2, ROWS, HALF), f32),
            dma((5,)),
            dma((STEPS, CHIPS)),
            dma((STEPS, CHIPS)),
            dma((STEPS, CHIPS)),
            dma((STEPS, CHIPS)),
            dma((STEPS, X)),
            dma((STEPS, X)),
            dma((STEPS, X - 1)),
            dma((STEPS, X - 1)),
            dma((STEPS, Z)),
            dma((STEPS, Z)),
            dma((STEPS, 2)),
            dma((STEPS, 2)),
        ],
        compiler_params=pltpu.CompilerParams(
            collective_id=0, has_side_effects=True, vmem_limit_bytes=48 * 1024 * 1024
        ),
        cost_estimate=pl.CostEstimate(
            flops=STEPS * 6 * USERS * BLOCK * R,
            bytes_accessed=4 * 1024 * 1024,
            transcendentals=0,
        ),
    )(*inputs)
    outs = [pltpu.with_memory_space_constraint(a, pltpu.VMEM) for a in outs]
    return pl.pallas_call(
        write_out,
        out_shape=(
            jax.ShapeDtypeStruct(users.shape, bf16),
            jax.ShapeDtypeStruct(items.shape, f32),
            jax.ShapeDtypeStruct(items.shape, f32),
        ),
        in_specs=[any_space] * 3,
        out_specs=(any_space,) * 3,
        scratch_shapes=[dma((3,))],
    )(*outs)


def solution(mesh):
    rows = P(("stratum", "user"), None)
    return jax.shard_map(
        local,
        mesh=mesh,
        in_specs=(rows, rows, rows, P(("stratum", "user"), None, None)),
        out_specs=(rows, rows, rows),
        check_vma=False,
    )
```

```python
import functools

import jax
import jax.numpy as jnp
from jax import lax
from jax.experimental import pallas as pl
from jax.experimental.pallas import tpu as pltpu
from jax.sharding import PartitionSpec as P

R = 512
HALF = 256
STEPS = 4
USERS = 1024
BLOCK = 256
X = 4
Z = 4
CHIPS = 16
ROWS = 16
STRATA = 16
FACTOR = R**-0.5
user_rate = 1.0
item_rate = 0.04
inertia = 0.6

MESH = pl.DeviceIdType.MESH
NT = (((1,), (1,)), ((), ()))
NN = (((1,), (0,)), ((), ()))
TILE = 256


def dot(a, b, dims):
    return lax.dot_general(a, b, dims, preferred_element_type=jnp.float32)


def kernel(
    users_in,
    items_in,
    momentum_in,
    ratings_in,
    users_out,
    items_out,
    momentum_out,
    u,
    raw,
    x,
    wide0,
    wide1,
    own,
    first,
    w,
    score,
    e,
    et,
    g,
    give,
    take,
    part,
    along_x,
    line,
    parts,
    state,
    fresh,
    load_sem,
    ag_send,
    ag_recv,
    fw_send,
    fw_recv,
    sib_send,
    sib_recv,
    x_send,
    x_recv,
    rs_send,
    rs_recv,
    st_send,
    st_recv,
):
    s = lax.axis_index("stratum")
    me = lax.axis_index("user")
    core = me % 2
    chip = me // 2
    mx, mz = chip // Z, chip % Z
    prev = (s + STRATA - 1) % STRATA
    nxt = (s + 1) % STRATA
    other = 1 - core

    def chip_at(dx, dz):
        return ((mx + dx) % X) * Z + (mz + dz) % Z

    def dev(k, c):
        return k * 2 + c

    middle = (mz - 1) * (mz - 2) == 0
    loads = [
        pltpu.make_async_copy(items_in, own.at[0], load_sem.at[0]),
        pltpu.make_async_copy(momentum_in, own.at[1], load_sem.at[1]),
        pltpu.make_async_copy(ratings_in, raw, load_sem.at[2]),
        pltpu.make_async_copy(users_in.at[:, pl.ds(0, HALF)], u.at[0], load_sem.at[3]),
        pltpu.make_async_copy(users_in.at[:, pl.ds(HALF, HALF)], u.at[1], load_sem.at[4]),
    ]

    far = [(dx, dz) for dx in (2, 1, 3, 0) for dz in (2, 1, 3, 0)]
    barrier = pltpu.get_barrier_semaphore()

    def hello(stratum, user):
        pl.semaphore_signal(barrier, inc=1, device_id=(stratum, user), device_id_type=MESH)

    hello(nxt, me)
    for dx, dz in far[:-1]:
        hello(s, dev(chip_at(dx, dz), core))
    hello(s, dev(chip, other))
    for copy in loads:
        copy.start()
    loads[0].wait()
    loads[1].wait()
    first[core, chip] = jnp.concatenate([own[0, :, :HALF], own[0, :, HALF:]], axis=0).astype(
        jnp.bfloat16
    )
    pl.semaphore_wait(barrier, CHIPS + 1)

    def remote(src, dst, send, recv, stratum, user):
        return pltpu.make_async_remote_copy(
            src_ref=src,
            dst_ref=dst,
            send_sem=send,
            recv_sem=recv,
            device_id=(stratum, user),
            device_id_type=MESH,
        )

    def lines_of(k):
        return pl.ds(pl.multiple_of(k * (Z * ROWS), Z * ROWS), Z * ROWS)

    def rows_of(k):
        return pl.ds(pl.multiple_of(k * ROWS, ROWS), ROWS)

    def finish(sends):
        for copy in sends:
            copy.wait_send()

    def pass_on(t, place, k):
        piece = place(core, k)
        copy = remote(piece, piece, fw_send.at[t, k], fw_recv.at[t, k], s, dev(chip, other))
        copy.start()
        return copy

    def spread(t, q, place, k):
        mine = place(core, k)
        sends = []
        for dx, dz in far[:-1]:
            to = dev(chip_at(dx, dz), core)
            sends.append(
                remote(mine, mine, ag_send.at[t, q, dx * Z + dz], ag_recv.at[t, k], s, to)
            )
            sends[-1].start()
        return sends

    def arrived(t, place, k):
        piece = place(core, k)
        remote(piece, piece, ag_send.at[t, 0, 0], ag_recv.at[t, k], s, me).wait_recv()

    def collect_passed(t, place):
        for dx, dz in far[::-1]:
            k = chip_at(dx, dz)
            piece = place(other, k)
            remote(piece, piece, fw_send.at[t, 0], fw_recv.at[t, k], s, me).wait_recv()

    def finish_passed(t, place):
        for k in range(CHIPS):
            piece = place(core, k)
            remote(piece, piece, fw_send.at[t, k], fw_recv.at[t, 0], s, me).wait_send()

    def place_first(c, k):
        return first.at[c, k]

    sends = spread(0, 0, place_first, chip)
    pass_on(0, place_first, chip)

    loads[2].wait()

    def split(i, _):
        r = pl.ds(pl.multiple_of(i * 128, 128), 128)
        for h, wide in enumerate((wide0, wide1)):
            lanes = slice(h * 128, h * 128 + 128)
            wide[...] = raw[r, :, lanes].astype(jnp.float32).reshape(128 * STEPS, 128)
        for t in range(STEPS):
            for h, wide in enumerate((wide0, wide1)):
                lanes = slice(h * 128, h * 128 + 128)
                x[t, r, lanes] = wide[pl.ds(t, 128, stride=STEPS), :].astype(jnp.bfloat16)
        return 0

    lax.fori_loop(0, USERS // 128, split, 0)
    loads[3].wait()
    loads[4].wait()

    for dx, dz in far[:-1][::-1]:
        k = chip_at(dx, dz)
        arrived(0, place_first, k)
        pass_on(0, place_first, k)
    collect_passed(0, place_first)
    finish(sends)
    finish_passed(0, place_first)
    pieces = [first[c].astype(jnp.float32).reshape(CHIPS, 2, 8, HALF) for c in range(2)]
    for h in range(2):
        w[0, h] = (
            jnp.concatenate([pieces[0][:, h : h + 1], pieces[1][:, h : h + 1]], axis=1)
            .reshape(BLOCK, HALF)
            .astype(jnp.bfloat16)
        )

    def eight(c):
        return pl.ds(pl.multiple_of(c * 8, 8), 8)

    def state_moves(t):
        if t == 0:
            to = mx * Z + 1 + mz // 2
            return [
                remote(
                    own.at[:, :, pl.ds(c * HALF, HALF)],
                    state.at[0, mz % 2, :, eight(core), :],
                    st_send.at[0, c],
                    st_recv.at[0, (mz % 2) * 2 + core],
                    prev,
                    dev(to, c),
                )
                for c in range(2)
            ]
        if t < STEPS - 1:
            return [
                remote(fresh.at[t - 1], state.at[t], st_send.at[t, 0], st_recv.at[t, 0], prev, me)
            ]
        return [
            remote(
                fresh.at[t - 1, q, :, pl.ds(c * 8, 8), :],
                state.at[t, 0, :, eight(core), :],
                st_send.at[t, q * 2 + c],
                st_recv.at[t, core],
                prev,
                dev(mx * Z + 2 * (mz - 1) + q, c),
            )
            for q in range(2)
            for c in range(2)
        ]

    def state_arrived(t):
        if t == 0:
            for q in range(2):
                for c in range(2):
                    remote(
                        own.at[:, :, pl.ds(0, HALF)],
                        state.at[0, q, :, pl.ds(c * 8, 8), :],
                        st_send.at[0, 0],
                        st_recv.at[0, q * 2 + c],
                        s,
                        me,
                    ).wait_recv()
        elif t < STEPS - 1:
            remote(
                fresh.at[t - 1], state.at[t], st_send.at[t, 0], st_recv.at[t, 0], s, me
            ).wait_recv()
        else:
            for c in range(2):
                remote(
                    fresh.at[t - 1, 0, :, pl.ds(c * 8, 8), :],
                    state.at[t, 0, :, pl.ds(c * 8, 8), :],
                    st_send.at[t, 0],
                    st_recv.at[t, c],
                    s,
                    me,
                ).wait_recv()

    def updated(t, q):
        for z_of in range(Z):
            remote(
                line.at[t, rows_of(0), :],
                parts.at[t, q, z_of],
                rs_send.at[t, 0],
                rs_recv.at[t, q, z_of],
                s,
                me,
            ).wait_recv()
        grads = jnp.sum(parts[t, q].astype(jnp.float32), axis=0)
        momentum = inertia * state[t, q, 1] + FACTOR * grads
        return state[t, q, 0] - item_rate * momentum, momentum

    for t in range(STEPS):
        last = t == STEPS - 1

        def place(c, k, t=t):
            return w.at[t, c, rows_of(k), :]

        tiles = [pl.ds(i * TILE, TILE) for i in range(USERS // TILE)]
        if t == 0:
            for copy in state_moves(0):
                copy.start()
            for r in tiles:
                score[r, :] = dot(u[core, r, :], w[t, core], NT)
        else:
            for r in tiles:
                score[r, :] = dot(u[core, r, :], w[t, core], NT)
            collect_passed(t, place)

            @pl.when(middle)
            def _(t=t):
                for copy in state_moves(t):
                    copy.start()
        for r in tiles:
            total = score[r, :] + dot(u[other, r, :], w[t, other], NT)
            tile = x[t, r, :].astype(jnp.float32)
            resid = jnp.where(tile != 0, total * FACTOR - tile, 0.0).astype(jnp.bfloat16)
            e[r, :] = resid
            et[:, r] = resid.T
        if last:
            for h in range(2):
                g[h] = dot(et[...], u[h], NN).reshape(CHIPS, 2, 8, HALF)

            def piece_for(c):
                both = [g[h, :, pl.ds(c, 1)] for h in range(2)]
                return jnp.concatenate(both, axis=1).reshape(BLOCK, HALF)

            give[t] = piece_for(other).astype(jnp.bfloat16)
        else:
            give[t] = dot(et[...], u[other], NN).astype(jnp.bfloat16)
        swaps = {}
        for dx in (2, 1, 3, 0):
            lines = lines_of((mx + dx) % X)
            swaps[dx] = remote(
                give.at[t, lines, :],
                take.at[t, lines, :],
                sib_send.at[t, dx],
                sib_recv.at[t, dx],
                s,
                dev(chip, other),
            )
            swaps[dx].start()
        if not last:
            g[0] = dot(et[...], u[core], NN).reshape(CHIPS, 2, 8, HALF)
        for h in range(2):
            for r in tiles:
                change = dot(e[r, :], w[t, h], NN)
                moved = (u[h, r, :].astype(jnp.float32) - user_rate * FACTOR * change).astype(
                    jnp.bfloat16
                )
                if last:
                    users_out[r, h * HALF : h * HALF + HALF] = moved
                else:
                    u[h, r, :] = moved

        def chip_sum(dx, t=t, last=last, swaps=swaps):
            x_of = (mx + dx) % X
            four = pl.ds(x_of * Z, Z)
            if last:
                both = [g[h, four, pl.ds(core, 1)] for h in range(2)]
                mine = jnp.concatenate(both, axis=1)
            else:
                mine = g[0, four]
            swaps[dx].wait_recv()
            return mine.reshape(Z * ROWS, HALF) + take[t, lines_of(x_of), :].astype(jnp.float32)

        gives = []
        for dx in (2, 1, 3):
            x_of = (mx + dx) % X
            part[t, lines_of(x_of), :] = chip_sum(dx).astype(jnp.bfloat16)
            gives.append(
                remote(
                    part.at[t, lines_of(x_of), :],
                    along_x.at[t, dx - 1],
                    x_send.at[t, dx - 1],
                    x_recv.at[t, dx - 1],
                    s,
                    dev(x_of * Z + mz, core),
                )
            )
            gives[-1].start()
        total = chip_sum(0)
        for i in (1, 2, 0):
            gives[(2, 1, 3).index(i + 1)].wait_recv()
            total += along_x[t, i].astype(jnp.float32)
        line[t] = total.astype(jnp.bfloat16)
        if last:
            to_owners = [(z_of, 0, z_of) for z_of in range(Z)]
        else:
            to_owners = [(2 * (m - 1) + q, q, m) for q in range(2) for m in (1, 2)]
        for i, (z_of, q, owner) in enumerate(to_owners):
            gives.append(
                remote(
                    line.at[t, pl.ds(z_of * ROWS, ROWS), :],
                    parts.at[t, q, mz],
                    rs_send.at[t, i],
                    rs_recv.at[t, q, mz],
                    prev,
                    dev(mx * Z + owner, core),
                )
            )
            gives[-1].start()
        groups = [(dx, m, q) for q in range(2) for dx in (2, 1, 3, 0) for m in (1, 2)]
        if last:
            state_arrived(t)
            items, momentum = updated(t, 0)
            for h in range(2):
                items_out[:, h * HALF : h * HALF + HALF] = items[h * 8 : h * 8 + 8]
                momentum_out[:, h * HALF : h * HALF + HALF] = momentum[h * 8 : h * 8 + 8]
        else:

            def place(c, k, t=t + 1):
                return w.at[t, c, rows_of(k), :]

            @pl.when(middle)
            def _(t=t, place=place):
                state_arrived(t)
                for q in range(2):
                    items, momentum = updated(t, q)
                    k = mx * Z + 2 * (mz - 1) + q
                    w[t + 1, core, rows_of(k), :] = items.astype(jnp.bfloat16)
                    spread(t + 1, q, place, k)
                    pass_on(t + 1, place, k)
                    fresh[t, q, 0] = items
                    fresh[t, q, 1] = momentum

            for dx, m, q in groups[::-1][8:] + groups[::-1][:8]:
                x_of = (mx + dx) % X
                k = x_of * Z + 2 * (m - 1) + q

                def take_in(k=k, t=t, place=place):
                    arrived(t + 1, place, k)
                    pass_on(t + 1, place, k)

                if dx == 0:
                    pl.when(mz != m)(take_in)
                else:
                    take_in()
        finish([*gives, *swaps.values()])

    finish(state_moves(0))

    @pl.when(middle)
    def _():
        for t in range(1, STEPS):
            finish(state_moves(t))
            for q in range(2):
                for dx, dz in far[:-1]:
                    mine = w.at[t, core, rows_of(0), :]
                    remote(
                        mine, mine, ag_send.at[t, q, dx * Z + dz], ag_recv.at[t, 0], s, me
                    ).wait_send()

    for t in range(1, STEPS):
        finish_passed(t, lambda c, k, t=t: w.at[t, c, rows_of(k), :])


def write_out(users, items, momentum, users_out, items_out, momentum_out, sem):
    copies = [
        pltpu.make_async_copy(users, users_out, sem.at[0]),
        pltpu.make_async_copy(items, items_out, sem.at[1]),
        pltpu.make_async_copy(momentum, momentum_out, sem.at[2]),
    ]
    for copy in copies:
        copy.start()
    for copy in copies:
        copy.wait()


def local(users, items, momentum, ratings):
    bf16, f32 = jnp.bfloat16, jnp.float32
    any_space = pl.BlockSpec(memory_space=pl.ANY)
    vmem = pl.BlockSpec(memory_space=pltpu.VMEM)
    dma = pltpu.SemaphoreType.DMA
    inputs = [
        pltpu.with_memory_space_constraint(a, pltpu.HBM) for a in (users, items, momentum, ratings)
    ]
    outs = pl.pallas_call(
        kernel,
        out_shape=(
            pltpu.VMEM(users.shape, bf16),
            pltpu.VMEM(items.shape, f32),
            pltpu.VMEM(items.shape, f32),
        ),
        in_specs=[any_space] * 4,
        out_specs=(vmem, vmem, vmem),
        scratch_shapes=[
            pltpu.VMEM((2, USERS, HALF), bf16),
            pltpu.VMEM((USERS, STEPS, BLOCK), bf16),
            pltpu.VMEM((STEPS, USERS, BLOCK), bf16),
            pltpu.VMEM((128 * STEPS, 128), f32),
            pltpu.VMEM((128 * STEPS, 128), f32),
            pltpu.VMEM((2, 8, R), f32),
            pltpu.VMEM((2, CHIPS, ROWS, HALF), bf16),
            pltpu.VMEM((STEPS, 2, BLOCK, HALF), bf16),
            pltpu.VMEM((USERS, BLOCK), f32),
            pltpu.VMEM((USERS, BLOCK), bf16),
            pltpu.VMEM((BLOCK, USERS), bf16),
            pltpu.VMEM((2, CHIPS, 2, 8, HALF), f32),
            pltpu.VMEM((STEPS, BLOCK, HALF), bf16),
            pltpu.VMEM((STEPS, BLOCK, HALF), bf16),
            pltpu.VMEM((STEPS, BLOCK, HALF), bf16),
            pltpu.VMEM((STEPS, X - 1, Z * ROWS, HALF), bf16),
            pltpu.VMEM((STEPS, Z * ROWS, HALF), bf16),
            pltpu.VMEM((STEPS, 2, Z, ROWS, HALF), bf16),
            pltpu.VMEM((STEPS, 2, 2, ROWS, HALF), f32),
            pltpu.VMEM((STEPS, 2, 2, ROWS, HALF), f32),
            dma((5,)),
            dma((STEPS, 2, CHIPS)),
            dma((STEPS, CHIPS)),
            dma((STEPS, CHIPS)),
            dma((STEPS, CHIPS)),
            dma((STEPS, X)),
            dma((STEPS, X)),
            dma((STEPS, X - 1)),
            dma((STEPS, X - 1)),
            dma((STEPS, Z)),
            dma((STEPS, 2, Z)),
            dma((STEPS, 4)),
            dma((STEPS, 4)),
        ],
        compiler_params=pltpu.CompilerParams(
            collective_id=0, has_side_effects=True, vmem_limit_bytes=48 * 1024 * 1024
        ),
        cost_estimate=pl.CostEstimate(
            flops=STEPS * 6 * USERS * BLOCK * R,
            bytes_accessed=4 * 1024 * 1024,
            transcendentals=0,
        ),
    )(*inputs)
    outs = [pltpu.with_memory_space_constraint(a, pltpu.VMEM) for a in outs]
    return pl.pallas_call(
        write_out,
        out_shape=(
            jax.ShapeDtypeStruct(users.shape, bf16),
            jax.ShapeDtypeStruct(items.shape, f32),
            jax.ShapeDtypeStruct(items.shape, f32),
        ),
        in_specs=[any_space] * 3,
        out_specs=(any_space,) * 3,
        scratch_shapes=[dma((3,))],
    )(*outs)


def solution(mesh):
    rows = P(("stratum", "user"), None)
    return jax.shard_map(
        local,
        mesh=mesh,
        in_specs=(rows, rows, rows, P(("stratum", "user"), None, None)),
        out_specs=(rows, rows, rows),
        check_vma=False,
    )
```
